512 devices in a mesh: dp: 128 (over z, x, core), mp: 4 (over y).
Axes of the slice: x: 4, y: 4, z: 16, core: 2. Of those that a mesh axis runs over, the one named last changes fastest.
Arguments:
- states: bfloat16 [32768, 2048], P('dp'), may hold values from -6 to 6
- inner_weights: bfloat16 [2, 2048, 3072], P(None, 'dp', 'mp'), may hold values from -0.125 to 0.125
- down_weight: bfloat16 [1024, 3072], P('dp', 'mp'), may hold values from -0.109375 to 0.109375
- cotangent: bfloat16 [32768, 1024], P('dp'), may hold values from -24 to 24
- routes: int32 [32768], P('dp'), may hold values from -1 to 127, as said below
Outputs:
- layer_output: bfloat16 [32768, 1024], P('dp', 'mp')
- grad_gates: bfloat16 [32768, 3072], P('dp', 'mp')
- grad_linear: bfloat16 [32768, 3072], P('dp', 'mp')
- down_grad: float32 [1024, 3072], P('dp', 'mp')
The draws below stay inside these ranges and needn't reach their ends.
Inputs may be any that keep to these rules, and one draw needn't show every extreme that they name: `routes`: -1 marks a dropped token; otherwise the data-axis index of the device that takes its row. Among the 256 rows of one data-axis index at most 2 kept rows name any one destination; one destination is named by exactly 2 kept rows of every index; every index keeps 2 rows or more.
All inputs are finite; a program needn't handle non-finite values.
Results may differ from the reference program's by a relative error of at most 0.013.
Values may be sent and summed in bfloat16 or wider, within the bound.
A program may use at most 64 MiB of HBM per device.

```python
import jax
import jax.numpy as jnp
from jax import lax

D = 2048
FW = 3072
DW = 1024
TOK_DEV = 256
CAP = 2
SLOTS = 256
TOKENS = 32768
N_DP = 128
N_MP = 4


def draw_routes(key, part):
    key = jax.random.fold_in(key, 11)
    slot_total = N_DP * CAP
    usable = min(TOK_DEV, slot_total)
    lowest = max(CAP, 3 * usable // 4)
    common = jax.random.randint(jax.random.fold_in(key, 1), (), 0, N_DP)

    def one_shard(shard):
        shard_key = jax.random.fold_in(jax.random.fold_in(key, 2), shard)
        order_key = jax.random.fold_in(shard_key, 1)
        count_key = jax.random.fold_in(shard_key, 2)
        place_key = jax.random.fold_in(shard_key, 3)
        shuffled = jax.random.permutation(order_key, slot_total).astype(jnp.int32)
        priority = jnp.where(shuffled // CAP == common, -1, jnp.arange(slot_total, dtype=jnp.int32))
        sequence = shuffled[jnp.argsort(priority, stable=True)]
        position = (jnp.arange(TOK_DEV, dtype=jnp.int32) % slot_total).astype(jnp.int32)
        targets = (sequence[position] // CAP).astype(jnp.int32)
        kept_count = jax.random.randint(count_key, (), lowest, usable + 1)
        values_kept = jnp.where(jnp.arange(TOK_DEV) < kept_count, targets, -1).astype(jnp.int32)
        placement = jax.random.permutation(place_key, TOK_DEV)
        return jnp.zeros((TOK_DEV,), jnp.int32).at[placement].set(values_kept)
    return jax.vmap(one_shard)(jnp.arange(N_DP)).reshape(TOKENS).astype(jnp.int32)


def with_spikes(result, rng, source, target, blocks, factor):
    def block_of(axis_at):
        return (jnp.arange(result.shape[axis_at]) // (result.shape[axis_at] // blocks)).reshape((-1,) + (1,) * (result.ndim - 1 - axis_at))

    first = jax.random.permutation(rng, blocks)[block_of(target)]
    second = (block_of(target) + blocks // 2) % blocks
    return jnp.where((block_of(source) == first) | (block_of(source) == second), factor * result, result)


def level_of(stream_key, dims, shards, smallest, largest):
    def one(dim, shards_of):
        heights = jax.random.uniform(jax.random.fold_in(jax.random.fold_in(stream_key, 6), dim), (shards_of,), jnp.float32, smallest / len(shards), largest / len(shards))
        return jnp.repeat(jnp.exp(heights), dims[dim] // shards_of).reshape((-1,) + (1,) * (len(dims) - dim - 1))

    gain = one(*shards[0])
    for cut in shards[1:]:
        gain = gain * one(*cut)
    return gain


def normal_values(stream_key, shape, spread, reach, cuts=(), kind=jnp.bfloat16):
    result = spread * jax.random.normal(stream_key, shape, jnp.float32)
    if cuts:
        result = result * level_of(stream_key, shape, cuts, -0.22, 0.18)
    return jnp.clip(result, -reach, reach).astype(kind)


def heavy_noise(rng, extent, scale, reach, pieces, heavy, held_as=jnp.bfloat16):
    result = scale * jax.random.normal(rng, extent, jnp.float32)
    if pieces:
        result = result * level_of(rng, extent, pieces, -0.22, 0.18)
    return jnp.clip(with_spikes(result, jax.random.fold_in(rng, 3), *heavy), -reach, reach).astype(held_as)


def setup_inputs(seed: int = 0) -> dict:
    arg_keys = jax.random.split(jax.random.key(seed), 6)
    states = normal_values(arg_keys[0], (TOKENS, D), 1.0, 6.0, ((0, 128),))
    inner_weights = normal_values(arg_keys[1], (2, D, FW), D ** -0.5, 0.125, ((1, 128), (2, 4)))
    down_weight = normal_values(arg_keys[2], (DW, FW), FW ** -0.5, 0.109375, ((0, 128), (1, 4)))
    cotangent = heavy_noise(arg_keys[3], (TOKENS, DW), 1.0, 24.0, ((0, 128),), (0, 1, 128, 5.5))
    routes = draw_routes(jax.random.fold_in(arg_keys[5], 71), 0)
    return {"states": states, "inner_weights": inner_weights, "down_weight": down_weight, "cotangent": cotangent, "routes": routes}


def reference(states, inner_weights, down_weight, cotangent, routes):
    block = FW // N_MP
    kept_rows = routes >= 0
    zero_value = jnp.zeros((), jnp.bfloat16)
    kept_cot = jnp.where(kept_rows[:, None], cotangent, zero_value)

    def shard_step(total, inputs):
        rows, cot_rows = inputs
        gate_pre = jnp.dot(rows, inner_weights[0], preferred_element_type=jnp.float32).astype(jnp.bfloat16)
        up_pre = jnp.dot(rows, inner_weights[1], preferred_element_type=jnp.float32).astype(jnp.bfloat16)
        gate_float = gate_pre.astype(jnp.float32)
        up_float = up_pre.astype(jnp.float32)
        sigmoid_gate = jax.nn.sigmoid(gate_float)
        active = gate_float * sigmoid_gate
        hidden = (active * up_float).astype(jnp.bfloat16)
        output_sum = jnp.zeros((rows.shape[0], DW), jnp.float32)
        for part_index in range(N_MP):
            piece = hidden[:, part_index * block:(part_index + 1) * block]
            weight_piece = down_weight[:, part_index * block:(part_index + 1) * block]
            partial_value = lax.optimization_barrier(jnp.dot(piece, weight_piece.T, preferred_element_type=jnp.float32).astype(jnp.bfloat16))
            output_sum = output_sum + partial_value.astype(jnp.float32)
        layer_rows = output_sum.astype(jnp.bfloat16)
        d_hidden = jnp.dot(cot_rows, down_weight, preferred_element_type=jnp.float32)
        gate_rows = (d_hidden * up_float * (sigmoid_gate * (1.0 + gate_float * (1.0 - sigmoid_gate)))).astype(jnp.bfloat16)
        up_rows = (d_hidden * active).astype(jnp.bfloat16)
        total = total + jnp.dot(cot_rows.T, hidden, preferred_element_type=jnp.float32)
        return total, (layer_rows, gate_rows, up_rows)

    state_blocks = states.reshape(N_DP, TOK_DEV, D)
    cot_blocks = kept_cot.reshape(N_DP, TOK_DEV, DW)
    down_grad, (layer_blocks, gate_blocks, up_blocks) = lax.scan(shard_step, jnp.zeros((DW, FW), jnp.float32), (state_blocks, cot_blocks))
    layer_output = layer_blocks.reshape(TOKENS, DW)

    route_blocks = routes.reshape(N_DP, TOK_DEV).astype(jnp.int32)
    targets = jnp.arange(N_DP, dtype=jnp.int32)
    onehot = (route_blocks[:, :, None] == targets[None, None, :]).astype(jnp.int32)
    earlier = jnp.cumsum(onehot, axis=1) - onehot
    slot_index = jnp.sum(earlier * onehot, axis=2).astype(jnp.int32)
    source = jnp.arange(N_DP, dtype=jnp.int32)[:, None]
    flat_index = route_blocks * SLOTS + source * CAP + slot_index
    flat_index = jnp.where(route_blocks >= 0, flat_index, N_DP * SLOTS).reshape(TOKENS).astype(jnp.int32)

    def place(values):
        empty = jnp.zeros((N_DP * SLOTS + 1, FW), jnp.bfloat16)
        return empty.at[flat_index].set(values.reshape(TOKENS, FW))[:N_DP * SLOTS]

    return layer_output, place(gate_blocks), place(up_blocks), down_grad
```

```python
import jax
import jax.numpy as jnp
from jax import lax
from jax.experimental import pallas as pl
from jax.experimental.pallas import tpu as pltpu
from jax.sharding import PartitionSpec as P

BF = jnp.bfloat16
F32 = jnp.float32
MESH = pl.DeviceIdType.MESH

NZ, NX, NY = 16, 4, 4
NQ = NX * 2
TOK = 256
D = 2048
HID = 768
DW = 1024
SQ = D // NY
CQ = DW // NY
WQ = SQ + CQ
TILE = 256
LAGX = 2
LAGS = 4


def z_offset(i):
    return -((i + 1) // 2) if i % 2 else i // 2


def goes_right(i):
    return i == 0 or (i % 2 == 1 and i < NZ - 1)


def kernel(
    routes_ref, states_ref, inner_ref, down_ref, cot_ref,
    layer_ref, gates_ref, linear_ref, dgrad_ref,
    w, dn, dsib, s_buf, r1, t_buf, r2, rows, hidden, ct, ctp32, ctp,
    p_send, p_recv, p_own, x_send, x_recv, x_own, z_send, z_recv, l_send, l_recv,
    sib0_s, sib0_r, zs, zr, xls, xlr, xrs, xrr, x2s, x2r, sbs, sbr,
    a1s, a1r, a2s, a2r, a3s, a3r, p0s, p0r, p1s, p1r, p2s, p2r, ls, lr,
):
    d, y = lax.axis_index("dp"), lax.axis_index("mp")
    c, x, z = lax.rem(d, 2), lax.rem(d // 2, NX), d // NQ
    q = lax.rem(d, NQ)

    def dev(zz, xx, cc):
        return ((zz * NX + xx) * 2 + cc, y)

    def plus(a, k, n):
        return lax.rem(a + (k + n), n)

    def remote(src, dst, send, recv, to):
        return pltpu.make_async_remote_copy(
            src_ref=src, dst_ref=dst, send_sem=send, recv_sem=recv, device_id=to, device_id_type=MESH
        )

    right, left = dev(z, plus(x, 1, NX), c), dev(z, plus(x, -1, NX), c)
    up, down = dev(plus(z, 1, NZ), x, c), dev(plus(z, -1, NZ), x, c)
    sibling = dev(z, x, 1 - c)

    barrier = pltpu.get_barrier_semaphore()
    for k in range(1, NZ):
        pl.semaphore_signal(barrier, inc=1, device_id=dev(plus(z, k, NZ), x, c), device_id_type=MESH)
    for k in range(1, NQ):
        qq = plus(q, k, NQ)
        pl.semaphore_signal(barrier, inc=1, device_id=(z * NQ + qq, y), device_id_type=MESH)
    for k in range(1, NY):
        pl.semaphore_signal(barrier, inc=1, device_id=(d, plus(y, k, NY)), device_id_type=MESH)
    pl.semaphore_wait(barrier, NZ + NQ + NY - 3)

    def chunk(zz, xx, lane):
        at = zz * NX + xx
        return (
            w.at[lane, pl.ds(pl.multiple_of(at * 32, 32), 32), :],
            dn.at[pl.ds(pl.multiple_of(at * 16, 16), 16), pl.ds(pl.multiple_of(lane * 384, 128), 384)],
        )

    def group(zz, lane):
        return (
            w.at[lane, pl.ds(pl.multiple_of(zz * 128, 128), 128), :],
            dn.at[pl.ds(pl.multiple_of(zz * 64, 64), 64), pl.ds(pl.multiple_of(lane * 384, 128), 384)],
        )

    def move(refs, send, recv, i, to):
        return [remote(r, r, send.at[j, i], recv.at[j, i], to) for j, r in enumerate(refs)]

    sends = []

    def start(copies):
        for one in copies:
            one.start()
        sends.extend(copies)

    def arrive(copies):
        for one in copies:
            one.wait_recv()

    own_row = pl.multiple_of((z * NX + x) * 32 + c * 16, 16)
    sib_copies = [
        remote(
            inner_ref.at[1 - c], w.at[1 - c, pl.ds(own_row, 16), :], sib0_s.at[0], sib0_r.at[0], sibling
        ),
        remote(down_ref, dsib, sib0_s.at[1], sib0_r.at[1], sibling),
    ]
    start(sib_copies)
    w[c, pl.ds(own_row, 16), :] = inner_ref[c]

    r_row = jnp.broadcast_to(routes_ref[...].astype(F32), (TOK, TOK))
    r_col = r_row.T
    sub = lax.broadcasted_iota(jnp.int32, (TOK, TOK), 0)
    lane_i = lax.broadcasted_iota(jnp.int32, (TOK, TOK), 1)
    before = jnp.where((r_row == r_col) & (sub < lane_i), 1.0, 0.0)
    count = jnp.sum(before, axis=0, keepdims=True)
    slot = jnp.where(r_row >= 0, r_row * 2.0 + count, -1.0)
    pick = jnp.where(slot == sub.astype(F32), 1.0, 0.0).astype(BF)
    part = jnp.dot(
        pick, states_ref[:, pl.ds(pl.multiple_of(y * SQ, SQ), SQ)], preferred_element_type=F32
    ).astype(BF)
    s_buf[:, :, :SQ] = part.reshape(NZ, 16, SQ)
    part = jnp.dot(
        pick, cot_ref[:, pl.ds(pl.multiple_of(y * CQ, CQ), CQ)], preferred_element_type=F32
    ).astype(BF)
    s_buf[:, :, SQ:] = part.reshape(NZ, 16, CQ)
    r1[pl.ds(z, 1)] = s_buf[pl.ds(z, 1)]

    theirs = [
        remote(
            inner_ref.at[c],
            w.at[c, pl.ds(pl.multiple_of((z * NX + x) * 32 + (1 - c) * 16, 16), 16), :],
            sib0_s.at[0],
            sib0_r.at[0],
            sibling,
        ),
        sib_copies[1],
    ]
    arrive(theirs)
    mine32, sib32 = down_ref[...].astype(F32), dsib[...].astype(F32)
    first, second = jnp.where(c == 0, mine32, sib32), jnp.where(c == 0, sib32, mine32)
    both = jnp.concatenate([first, second], axis=0)
    both = jnp.where(c == 0, both[:, :384], both[:, 384:]).astype(BF)
    dn[
        pl.ds(pl.multiple_of((z * NX + x) * 16, 16), 16), pl.ds(pl.multiple_of(c * 384, 128), 384)
    ] = both

    def send_z(i):
        own = chunk(plus(z, z_offset(i), NZ), x, c)
        if i == 0:
            start(move(own, zs, zr, 1, up))
            start(move(own, zs, zr, 2, down))
        elif i % 2 and i + 2 < NZ:
            start(move(own, zs, zr, i + 2, up))
        elif i % 2 == 0 and i + 2 < NZ - 1:
            start(move(own, zs, zr, i + 2, down))

    def send_x(i):
        own = chunk(plus(z, z_offset(i), NZ), x, c)
        start(move(own, xls, xlr, i, right))
        start(move(own, xrs, xrr, i, left))

    def pass_x(i):
        zz = plus(z, z_offset(i), NZ)
        from_left, from_right = chunk(zz, plus(x, -1, NX), c), chunk(zz, plus(x, 1, NX), c)
        arrive(move(from_left, xls, xlr, i, right))
        arrive(move(from_right, xrs, xrr, i, left))
        if goes_right(i):
            start(move(from_left, x2s, x2r, i, right))
        else:
            start(move(from_right, x2s, x2r, i, left))

    def to_sibling(i):
        zz = plus(z, z_offset(i), NZ)
        arrive(move(chunk(zz, plus(x, 2, NX), c), x2s, x2r, i, right))
        start(move(group(zz, c), sbs, sbr, i, sibling))

    def rows_z(k):
        to = plus(z, k, NZ)
        start([remote(s_buf.at[to], r1.at[z], a1s.at[k], a1r.at[k], dev(to, x, c))])

    def permuted(values, out_first):
        low = sub % out_first
        src = (low // 2) * (TOK // (out_first // 2)) + (sub // out_first) * 2 + sub % 2
        matrix = jnp.where(src == lane_i, 1.0, 0.0).astype(BF)
        return jnp.dot(matrix, values, preferred_element_type=F32).astype(BF)

    def rows_q():
        for k in range(1, NZ):
            at = plus(z, -k, NZ)
            arrive([remote(s_buf.at[at], r1.at[at], a1s.at[k], a1r.at[k], dev(at, x, c))])
        t_buf[...] = permuted(r1[...].reshape(TOK, WQ), 32).reshape(NQ, 32, WQ)
        r2[pl.ds(q, 1)] = t_buf[pl.ds(q, 1)]
        for k in range(1, NQ):
            to = plus(q, k, NQ)
            start([remote(t_buf.at[to], r2.at[q], a2s.at[k], a2r.at[k], (z * NQ + to, y))])

    def rows_y():
        for k in range(1, NQ):
            at = plus(q, -k, NQ)
            arrive([remote(t_buf.at[at], r2.at[at], a2s.at[k], a2r.at[k], (z * NQ + at, y))])
        rows[pl.ds(y, 1)] = permuted(r2[...].reshape(TOK, WQ), 16).reshape(1, TOK, WQ)
        for k in range(1, NY):
            start([remote(rows.at[y], rows.at[y], a3s.at[k], a3r.at[k], (d, plus(y, k, NY)))])

    def rows_done():
        for k in range(1, NY):
            at = plus(y, -k, NY)
            arrive([remote(rows.at[at], rows.at[at], a3s.at[k], a3r.at[k], (d, at))])

    def transpose_cot():
        keep = r_col >= 0
        for j in range(DW // TILE):
            cols = slice(j * TILE, (j + 1) * TILE)
            ct[cols, :] = jnp.where(keep, cot_ref[:, cols].astype(F32), 0.0).T

        def one(n, carry):
            zz, xx, cc = n // NQ, (n // 2) % NX, n % 2
            to = (cc * NX + xx) * NZ + zz
            ctp32[pl.ds(pl.multiple_of(to * 8, 8), 8), :] = ct[pl.ds(pl.multiple_of(n * 8, 8), 8), :]
            return carry

        lax.fori_loop(0, NZ * NQ, one, 0)
        ctp[...] = ctp32[...].astype(BF)

    for i in range(NZ + LAGS):
        if i < NZ:
            if i > 0:
                arrive(move(chunk(plus(z, z_offset(i), NZ), x, c), zs, zr, i, up))
            send_z(i)
            send_x(i)
        if i < 8:
            for k in (2 * i + 1, 2 * i + 2):
                if k < NZ:
                    rows_z(k)
        if 0 <= i - LAGX < NZ:
            pass_x(i - LAGX)
        if 0 <= i - LAGS < NZ:
            to_sibling(i - LAGS)
        if i == 3:
            transpose_cot()
        if i == 10:
            rows_q()
        if i == 14:
            rows_y()
    for i in range(NZ):
        arrive(move(group(plus(z, z_offset(i), NZ), 1 - c), sbs, sbr, i, sibling))

    def preacts(gate_f32, up_f32):
        gate = gate_f32.astype(BF).astype(F32)
        up_value = up_f32.astype(BF).astype(F32)
        sig = jax.nn.sigmoid(gate)
        return gate, up_value, sig, gate * sig

    def columns(t):
        return pl.ds(pl.multiple_of(t * TILE, TILE), TILE)

    def forward(t, carry):
        cols = columns(t)
        _, up_value, _, active = preacts(
            jnp.dot(states_ref[...], w[0, :, cols], preferred_element_type=F32),
            jnp.dot(states_ref[...], w[1, :, cols], preferred_element_type=F32),
        )
        hidden[:, cols] = (active * up_value).astype(BF)
        return carry

    lax.fori_loop(0, HID // TILE, forward, 0)

    half = DW // 2

    def other_half(m, carry):
        at = pl.multiple_of((1 - c) * half + m * TILE, TILE)
        p_send[pl.ds(pl.multiple_of(m * TILE, TILE), TILE), :] = jnp.dot(
            ctp[pl.ds(at, TILE), :], hidden[...], preferred_element_type=F32
        ).astype(BF)
        return carry

    lax.fori_loop(0, half // TILE, other_half, 0)
    to_other = [remote(p_send, p_recv, p0s.at[0], p0r.at[0], sibling)]
    start(to_other)

    def layer_part(yy):
        return lax.dot_general(
            hidden[...],
            dn[pl.ds(pl.multiple_of(yy * TILE, TILE), TILE), :],
            (((1,), (1,)), ((), ())),
            preferred_element_type=F32,
        ).astype(BF)

    layer_copies = []
    for k in range(1, NY):
        to = plus(y, k, NY)
        l_send[k] = layer_part(to)
        layer_copies.append(remote(l_send.at[k], l_recv.at[k], ls.at[k], lr.at[k], (d, to)))
        start(layer_copies[-1:])
    l_send[0] = layer_part(y)

    def own_half(m, carry):
        at = pl.multiple_of(c * half + m * TILE, TILE)
        p_own[pl.ds(pl.multiple_of(m * TILE, TILE), TILE), :] = jnp.dot(
            ctp[pl.ds(at, TILE), :], hidden[...], preferred_element_type=F32
        )
        return carry

    lax.fori_loop(0, half // TILE, own_half, 0)
    arrive(to_other)
    x_copies = []
    for k in range(1, NX):
        to = plus(x, k, NX)
        at = pl.ds(pl.multiple_of(to * 128, 128), 128)
        x_send[k] = (p_own[at, :] + p_recv[at, :].astype(F32)).astype(BF)
        x_copies.append(remote(x_send.at[k], x_recv.at[k], p1s.at[k], p1r.at[k], dev(z, to, c)))
        start(x_copies[-1:])
    at = pl.ds(pl.multiple_of(x * 128, 128), 128)
    x_own[...] = p_own[at, :] + p_recv[at, :].astype(F32)

    rows_done()

    def backward(t, carry):
        cols = columns(t)
        gate = jnp.zeros((TOK, TILE), F32)
        up_value = jnp.zeros((TOK, TILE), F32)
        d_hidden = jnp.zeros((TOK, TILE), F32)
        for yy in range(NY):
            gate += jnp.dot(
                rows[yy, :, :SQ], w[0, yy * SQ : (yy + 1) * SQ, cols], preferred_element_type=F32
            )
            up_value += jnp.dot(
                rows[yy, :, :SQ], w[1, yy * SQ : (yy + 1) * SQ, cols], preferred_element_type=F32
            )
            d_hidden += jnp.dot(
                rows[yy, :, SQ:], dn[yy * CQ : (yy + 1) * CQ, cols], preferred_element_type=F32
            )
        gate, up_value, sig, active = preacts(gate, up_value)
        gates_ref[:, cols] = (d_hidden * up_value * (sig * (1.0 + gate * (1.0 - sig)))).astype(BF)
        linear_ref[:, cols] = (d_hidden * active).astype(BF)
        return carry

    lax.fori_loop(0, 1, backward, 0)

    arrive(x_copies)
    x_own[...] = (
        x_own[...] + x_recv[1].astype(F32) + x_recv[2].astype(F32) + x_recv[3].astype(F32)
    )
    z_copies = []
    for k in range(1, NZ):
        to = plus(z, k, NZ)
        piece = x_own[pl.ds(pl.multiple_of(to * 8, 8), 8), :]
        z_send[k] = jnp.concatenate([piece[:, :384], piece[:, 384:]], axis=0).astype(BF)
        z_copies.append(remote(z_send.at[k], z_recv.at[k], p2s.at[k], p2r.at[k], dev(to, x, c)))
        start(z_copies[-1:])

    lax.fori_loop(1, HID // TILE, backward, 0)

    arrive(layer_copies)
    layer_ref[...] = (
        l_send[0].astype(F32)
        + l_recv[1].astype(F32)
        + l_recv[2].astype(F32)
        + l_recv[3].astype(F32)
    ).astype(BF)

    arrive(z_copies)
    total = z_recv[1].astype(F32)
    for k in range(2, NZ):
        total += z_recv[k].astype(F32)
    mine = x_own[pl.ds(pl.multiple_of(z * 8, 8), 8), :]
    dgrad_ref[:, :384] = mine[:, :384] + total[:8]
    dgrad_ref[:, 384:] = mine[:, 384:] + total[8:]

    for one in sends:
        one.wait_send()


def body(states, inner_weights, down_weight, cotangent, routes):
    dma = lambda *shape: pltpu.SemaphoreType.DMA(shape)
    vm = lambda shape, kind=BF: pltpu.VMEM(shape, kind)
    return pl.pallas_call(
        kernel,
        out_shape=(
            jax.ShapeDtypeStruct((TOK, DW // NY), BF),
            jax.ShapeDtypeStruct((TOK, HID), BF),
            jax.ShapeDtypeStruct((TOK, HID), BF),
            jax.ShapeDtypeStruct((DW // 128, HID), F32),
        ),
        in_specs=[pl.BlockSpec(memory_space=pltpu.VMEM)] * 5,
        out_specs=tuple(pl.BlockSpec(memory_space=pltpu.VMEM) for _ in range(4)),
        scratch_shapes=[
            vm((2, D, HID)),
            vm((DW, HID)),
            vm((8, HID)),
            vm((NZ, 16, WQ)),
            vm((NZ, 16, WQ)),
            vm((NQ, 32, WQ)),
            vm((NQ, 32, WQ)),
            vm((NY, TOK, WQ)),
            vm((TOK, HID)),
            vm((DW, TOK), F32),
            vm((DW, TOK), F32),
            vm((DW, TOK)),
            vm((DW // 2, HID)),
            vm((DW // 2, HID)),
            vm((DW // 2, HID), F32),
            vm((NX, 128, HID)),
            vm((NX, 128, HID)),
            vm((128, HID), F32),
            vm((NZ, 16, HID // 2)),
            vm((NZ, 16, HID // 2)),
            vm((NY, TOK, DW // NY)),
            vm((NY, TOK, DW // NY)),
            dma(2),
            dma(2),
        ]
        + [dma(2, NZ)] * 10
        + [dma(NZ), dma(NZ), dma(NQ), dma(NQ), dma(NY), dma(NY)]
        + [dma(1), dma(1), dma(NX), dma(NX), dma(NZ), dma(NZ), dma(NY), dma(NY)],
        compiler_params=pltpu.CompilerParams(
            collective_id=0, has_side_effects=True, vmem_limit_bytes=48 * 1024 * 1024
        ),
    )(routes.reshape(1, TOK), states, inner_weights, down_weight, cotangent)


def solution(mesh):
    return jax.shard_map(
        body,
        mesh=mesh,
        in_specs=(P("dp", None), P(None, "dp", "mp"), P("dp", "mp"), P("dp", None), P("dp")),
        out_specs=(P("dp", "mp"), P("dp", "mp"), P("dp", "mp"), P("dp", "mp")),
        check_vma=False,
    )
```

```python
import jax
import jax.numpy as jnp
from jax import lax
from jax.experimental import pallas as pl
from jax.experimental.pallas import tpu as pltpu
from jax.sharding import PartitionSpec as P

BF = jnp.bfloat16
F32 = jnp.float32
MESH = pl.DeviceIdType.MESH

NZ, NX, NY = 16, 4, 4
NQ = NX * 2
TOK = 256
D = 2048
HID = 768
DW = 1024
SQ = D // NY
CQ = DW // NY
TILE = 256

ORDER = (0, -1, 1, -2, 2, -3, 3, -4, 4, -5, 5, -6, 6, -7, 7, 8)
NEXT = {0: ((1, -1), (-1, 1)), -7: ((1, 8),)}
for _k in range(1, 7):
    NEXT[-_k] = ((1, -_k - 1),)
    NEXT[_k] = ((-1, _k + 1),)
PIECES = 3
AT_Q, AT_Y = (10, 15, 20), (15, 20, 21)
PER_STEP = 3
FAR = [k for j in range(1, NZ // 2) for k in (j, NZ - j)] + [NZ // 2]
TURN = 4
LAGX = 2
LAGS = 4
LAGD = 3
LAST = NZ + 4


def goes_right(i):
    return ORDER[i] <= 0


def kernel(
    routes_in, states_in, inner_in, down_in, cot_in,
    layer_ref, gates_ref, linear_ref, dgrad_ref,
    routes_ref, states_ref, inner_ref, down_ref, cot_ref, in_sem,
    w, dn, dsib, s_buf, r1, t_buf, r2, rows, hidden, ct, ctp32, ctp,
    p_send, p_recv, p_own, x_send, x_recv, x_own, z_send, z_recv, l_send, l_recv,
    sib0_s, sib0_r, zs, zr, xls, xlr, xrs, xrr, x2s, x2r, sbs, sbr, dxs, dxr, dzs, dzr, dss, dsr,
    a1s, a1r, a2s, a2r, a3s, a3r, p0s, p0r, p1s, p1r, p2s, p2r, ls, lr,
):
    d, y = lax.axis_index("dp"), lax.axis_index("mp")
    c, x, z = lax.rem(d, 2), lax.rem(d // 2, NX), d // NQ
    q = lax.rem(d, NQ)

    def dev(zz, xx, cc):
        return ((zz * NX + xx) * 2 + cc, y)

    def plus(a, k, n):
        return lax.rem(a + (k + n), n)

    def remote(src, dst, send, recv, to):
        return pltpu.make_async_remote_copy(
            src_ref=src, dst_ref=dst, send_sem=send, recv_sem=recv, device_id=to, device_id_type=MESH
        )

    right, left = dev(z, plus(x, 1, NX), c), dev(z, plus(x, -1, NX), c)
    sibling = dev(z, x, 1 - c)

    pairs = (
        (inner_in, inner_ref),
        (down_in, down_ref),
        (routes_in, routes_ref),
        (states_in, states_ref),
        (cot_in, cot_ref),
    )
    loads = [pltpu.make_async_copy(a, b, in_sem.at[i]) for i, (a, b) in enumerate(pairs)]
    for one in loads:
        one.start()

    barrier = pltpu.get_barrier_semaphore()
    for k in range(1, NZ):
        pl.semaphore_signal(barrier, inc=1, device_id=dev(plus(z, k, NZ), x, c), device_id_type=MESH)
    for k in range(1, NQ):
        qq = plus(q, k, NQ)
        pl.semaphore_signal(barrier, inc=1, device_id=(z * NQ + qq, y), device_id_type=MESH)
    for k in range(1, NY):
        pl.semaphore_signal(barrier, inc=1, device_id=(d, plus(y, k, NY)), device_id_type=MESH)
    pl.semaphore_wait(barrier, NZ + NQ + NY - 3)

    def chunk(zz, xx, lane):
        return w.at[lane, pl.ds(pl.multiple_of((zz * NX + xx) * 32, 32), 32), :]

    def group(zz, lane):
        return w.at[lane, pl.ds(pl.multiple_of(zz * 128, 128), 128), :]

    def lanes(lane):
        return pl.ds(pl.multiple_of(lane * 384, 128), 384)

    def down_chunk(xx):
        return dn.at[pl.ds(pl.multiple_of((z * NX + xx) * 16, 16), 16), lanes(c)]

    def down_group(zz, lane):
        return dn.at[pl.ds(pl.multiple_of(zz * 64, 64), 64), lanes(lane)]

    def move(ref, send, recv, i, to):
        return [remote(ref, ref, send.at[i], recv.at[i], to)]

    sends = []

    def start(copies):
        for one in copies:
            one.start()
        sends.extend(copies)

    def arrive(copies):
        for one in copies:
            one.wait_recv()

    loads[0].wait()
    loads[1].wait()
    own_row = pl.multiple_of((z * NX + x) * 32 + c * 16, 16)
    sib_copies = [
        remote(
            inner_ref.at[1 - c], w.at[1 - c, pl.ds(own_row, 16), :], sib0_s.at[0], sib0_r.at[0], sibling
        ),
        remote(down_ref, dsib, sib0_s.at[1], sib0_r.at[1], sibling),
    ]
    start(sib_copies)
    w[c, pl.ds(own_row, 16), :] = inner_ref[c]

    for one in loads[2:]:
        one.wait()
    r_row = jnp.broadcast_to(routes_ref[...].astype(F32), (TOK, TOK))
    r_col = r_row.T
    sub = lax.broadcasted_iota(jnp.int32, (TOK, TOK), 0)
    lane_i = lax.broadcasted_iota(jnp.int32, (TOK, TOK), 1)
    before = jnp.where((r_row == r_col) & (sub < lane_i), 1.0, 0.0)
    count = jnp.sum(before, axis=0, keepdims=True)
    slot = jnp.where(r_row >= 0, r_row * 2.0 + count, -1.0)
    pick = jnp.where(slot == sub.astype(F32), 1.0, 0.0).astype(BF)
    for p in range(PIECES):
        if p < 2:
            values = states_ref[:, pl.ds(pl.multiple_of(y * SQ + p * TILE, TILE), TILE)]
        else:
            values = cot_ref[:, pl.ds(pl.multiple_of(y * CQ, CQ), CQ)]
        part = jnp.dot(pick, values, preferred_element_type=F32).astype(BF)
        s_buf[p] = part.reshape(NZ, 16, TILE)
        r1[p, pl.ds(z, 1)] = s_buf[p, pl.ds(z, 1)]

    theirs = [
        remote(
            inner_ref.at[c],
            w.at[c, pl.ds(pl.multiple_of((z * NX + x) * 32 + (1 - c) * 16, 16), 16), :],
            sib0_s.at[0],
            sib0_r.at[0],
            sibling,
        ),
        sib_copies[1],
    ]
    arrive(theirs)
    mine32, sib32 = down_ref[...].astype(F32), dsib[...].astype(F32)
    first, second = jnp.where(c == 0, mine32, sib32), jnp.where(c == 0, sib32, mine32)
    both = jnp.concatenate([first, second], axis=0)
    both = jnp.where(c == 0, both[:, :384], both[:, 384:]).astype(BF)
    dn[pl.ds(pl.multiple_of((z * NX + x) * 16, 16), 16), lanes(c)] = both

    def send_z(ref, send, recv, i):
        for step, there in NEXT.get(ORDER[i], ()):
            start(move(ref, send, recv, ORDER.index(there), dev(plus(z, step, NZ), x, c)))

    def send_x(i):
        own = chunk(plus(z, ORDER[i], NZ), x, c)
        start(move(own, xls, xlr, i, right))
        start(move(own, xrs, xrr, i, left))

    def pass_x(i):
        zz = plus(z, ORDER[i], NZ)
        from_left, from_right = chunk(zz, plus(x, -1, NX), c), chunk(zz, plus(x, 1, NX), c)
        arrive(move(from_left, xls, xlr, i, right))
        arrive(move(from_right, xrs, xrr, i, left))
        if goes_right(i):
            start(move(from_left, x2s, x2r, i, right))
        else:
            start(move(from_right, x2s, x2r, i, left))

    def to_sibling(i):
        zz = plus(z, ORDER[i], NZ)
        arrive(move(chunk(zz, plus(x, 2, NX), c), x2s, x2r, i, right))
        start(move(group(zz, c), sbs, sbr, i, sibling))

    onward = 1 - 2 * c

    def down_x():
        start(move(down_chunk(x), dxs, dxr, 0, right))
        start(move(down_chunk(x), dxs, dxr, 1, left))

    def down_x2():
        arrive(move(down_chunk(plus(x, -1, NX)), dxs, dxr, 0, right))
        arrive(move(down_chunk(plus(x, 1, NX)), dxs, dxr, 1, left))
        start(move(down_chunk(plus(x, -onward, NX)), dxs, dxr, 2, dev(z, plus(x, onward, NX), c)))

    def down_z(i):
        ref = down_group(plus(z, ORDER[i], NZ), c)
        if i == 0:
            arrive(move(down_chunk(plus(x, 2, NX)), dxs, dxr, 2, right))
        else:
            arrive(move(ref, dzs, dzr, i, right))
        send_z(ref, dzs, dzr, i)
        start(move(ref, dss, dsr, i, sibling))

    def rows_z(i):
        for n in range(i * PER_STEP, min((i + 1) * PER_STEP, PIECES * (NZ - 1))):
            p, k = n // (NZ - 1), FAR[n % (NZ - 1)]
            to = plus(z, k, NZ)
            start([remote(s_buf.at[p, to], r1.at[p, z], a1s.at[p, k], a1r.at[p, k], dev(to, x, c))])

    def permuted(values, out_first):
        low = sub % out_first
        src = (low // 2) * (TOK // (out_first // 2)) + (sub // out_first) * 2 + sub % 2
        matrix = jnp.where(src == lane_i, 1.0, 0.0).astype(BF)
        return jnp.dot(matrix, values, preferred_element_type=F32).astype(BF)

    def rows_q(p):
        for k in range(1, NZ):
            at = plus(z, -k, NZ)
            arrive([remote(s_buf.at[p, at], r1.at[p, at], a1s.at[p, k], a1r.at[p, k], dev(at, x, c))])
        t_buf[p] = permuted(r1[p].reshape(TOK, TILE), 32).reshape(NQ, 32, TILE)
        r2[p, pl.ds(q, 1)] = t_buf[p, pl.ds(q, 1)]
        for k in range(1, NQ):
            to = plus(q, k, NQ)
            start([remote(t_buf.at[p, to], r2.at[p, q], a2s.at[p, k], a2r.at[p, k], (z * NQ + to, y))])

    def rows_y(p):
        for k in range(1, NQ):
            at = plus(q, -k, NQ)
            arrive([remote(t_buf.at[p, at], r2.at[p, at], a2s.at[p, k], a2r.at[p, k], (z * NQ + at, y))])
        rows[p, pl.ds(y, 1)] = permuted(r2[p].reshape(TOK, TILE), 16).reshape(1, TOK, TILE)
        for k in range(1, NY):
            mine = rows.at[p, y]
            start([remote(mine, mine, a3s.at[p, k], a3r.at[p, k], (d, plus(y, k, NY)))])

    def rows_step(i):
        if i in AT_Q:
            rows_q(AT_Q.index(i))
        if i in AT_Y:
            rows_y(AT_Y.index(i))

    def rows_done():
        for p in range(PIECES):
            for k in range(1, NY):
                at = plus(y, -k, NY)
                arrive([remote(rows.at[p, at], rows.at[p, at], a3s.at[p, k], a3r.at[p, k], (d, at))])

    def transpose_cot():
        keep = r_col >= 0
        for j in range(DW // TILE):
            cols = slice(j * TILE, (j + 1) * TILE)
            ct[cols, :] = jnp.where(keep, cot_ref[:, cols].astype(F32), 0.0).T

        def one(n, carry):
            zz, xx, cc = n // NQ, (n // 2) % NX, n % 2
            to = (cc * NX + xx) * NZ + zz
            ctp32[pl.ds(pl.multiple_of(to * 8, 8), 8), :] = ct[pl.ds(pl.multiple_of(n * 8, 8), 8), :]
            return carry

        lax.fori_loop(0, NZ * NQ, one, 0)
        ctp[...] = ctp32[...].astype(BF)

    for i in range(LAST):
        if i < NZ:
            ref = chunk(plus(z, ORDER[i], NZ), x, c)
            if i > 0:
                arrive(move(ref, zs, zr, i, right))
            send_z(ref, zs, zr, i)
            send_x(i)
        if i == 0:
            down_x()
        if i == 1:
            down_x2()
        rows_z(i)
        if 0 <= i - LAGX < NZ:
            pass_x(i - LAGX)
        if 0 <= i - LAGD < NZ:
            down_z(i - LAGD)
        if 0 <= i - LAGS < NZ:
            to_sibling(i - LAGS)
        if i == TURN:
            transpose_cot()
        rows_step(i)
    for i in range(NZ):
        arrive(move(group(plus(z, ORDER[i], NZ), 1 - c), sbs, sbr, i, sibling))

    rows_step(LAST)

    def preacts(gate_f32, up_f32):
        gate = gate_f32.astype(BF).astype(F32)
        up_value = up_f32.astype(BF).astype(F32)
        sig = jax.nn.sigmoid(gate)
        return gate, up_value, sig, gate * sig

    def columns(t):
        return pl.ds(pl.multiple_of(t * TILE, TILE), TILE)

    def forward(t, carry):
        cols = columns(t)
        _, up_value, _, active = preacts(
            jnp.dot(states_ref[...], w[0, :, cols], preferred_element_type=F32),
            jnp.dot(states_ref[...], w[1, :, cols], preferred_element_type=F32),
        )
        hidden[:, cols] = (active * up_value).astype(BF)
        return carry

    lax.fori_loop(0, HID // TILE, forward, 0)

    rows_step(LAST + 1)

    half = DW // 2

    def other_half(m, carry):
        at = pl.multiple_of((1 - c) * half + m * TILE, TILE)
        p_send[pl.ds(pl.multiple_of(m * TILE, TILE), TILE), :] = jnp.dot(
            ctp[pl.ds(at, TILE), :], hidden[...], preferred_element_type=F32
        ).astype(BF)
        return carry

    lax.fori_loop(0, half // TILE, other_half, 0)
    to_other = [remote(p_send, p_recv, p0s.at[0], p0r.at[0], sibling)]
    start(to_other)

    for i in range(NZ):
        arrive(move(down_group(plus(z, ORDER[i], NZ), 1 - c), dss, dsr, i, sibling))

    def layer_part(yy):
        return lax.dot_general(
            hidden[...],
            dn[pl.ds(pl.multiple_of(yy * TILE, TILE), TILE), :],
            (((1,), (1,)), ((), ())),
            preferred_element_type=F32,
        ).astype(BF)

    layer_copies = []
    for k in range(1, NY):
        to = plus(y, k, NY)
        l_send[k] = layer_part(to)
        layer_copies.append(remote(l_send.at[k], l_recv.at[k], ls.at[k], lr.at[k], (d, to)))
        start(layer_copies[-1:])
    l_send[0] = layer_part(y)

    rows_step(LAST + 2)

    def own_half(m, carry):
        at = pl.multiple_of(c * half + m * TILE, TILE)
        p_own[pl.ds(pl.multiple_of(m * TILE, TILE), TILE), :] = jnp.dot(
            ctp[pl.ds(at, TILE), :], hidden[...], preferred_element_type=F32
        )
        return carry

    lax.fori_loop(0, half // TILE, own_half, 0)
    arrive(to_other)
    x_copies = []
    for k in range(1, NX):
        to = plus(x, k, NX)
        at = pl.ds(pl.multiple_of(to * 128, 128), 128)
        x_send[k] = (p_own[at, :] + p_recv[at, :].astype(F32)).astype(BF)
        x_copies.append(remote(x_send.at[k], x_recv.at[k], p1s.at[k], p1r.at[k], dev(z, to, c)))
        start(x_copies[-1:])
    at = pl.ds(pl.multiple_of(x * 128, 128), 128)
    x_own[...] = p_own[at, :] + p_recv[at, :].astype(F32)

    rows_step(LAST + 3)

    rows_done()

    def backward(t, carry):
        cols = columns(t)
        gate = jnp.zeros((TOK, TILE), F32)
        up_value = jnp.zeros((TOK, TILE), F32)
        d_hidden = jnp.zeros((TOK, TILE), F32)
        for yy in range(NY):
            for p in range(2):
                at = slice(yy * SQ + p * TILE, yy * SQ + (p + 1) * TILE)
                gate += jnp.dot(rows[p, yy], w[0, at, cols], preferred_element_type=F32)
                up_value += jnp.dot(rows[p, yy], w[1, at, cols], preferred_element_type=F32)
            at = slice(yy * CQ, (yy + 1) * CQ)
            d_hidden += jnp.dot(rows[2, yy], dn[at, cols], preferred_element_type=F32)
        gate, up_value, sig, active = preacts(gate, up_value)
        gates_ref[:, cols] = (d_hidden * up_value * (sig * (1.0 + gate * (1.0 - sig)))).astype(BF)
        linear_ref[:, cols] = (d_hidden * active).astype(BF)
        return carry

    lax.fori_loop(0, 1, backward, 0)

    arrive(x_copies)
    x_own[...] = (
        x_own[...] + x_recv[1].astype(F32) + x_recv[2].astype(F32) + x_recv[3].astype(F32)
    )
    z_copies = []
    for k in range(1, NZ):
        to = plus(z, k, NZ)
        piece = x_own[pl.ds(pl.multiple_of(to * 8, 8), 8), :]
        z_send[k] = jnp.concatenate([piece[:, :384], piece[:, 384:]], axis=0).astype(BF)
        z_copies.append(remote(z_send.at[k], z_recv.at[k], p2s.at[k], p2r.at[k], dev(to, x, c)))
        start(z_copies[-1:])

    lax.fori_loop(1, HID // TILE, backward, 0)

    arrive(layer_copies)
    layer_ref[...] = (
        l_send[0].astype(F32)
        + l_recv[1].astype(F32)
        + l_recv[2].astype(F32)
        + l_recv[3].astype(F32)
    ).astype(BF)

    arrive(z_copies)
    total = z_recv[1].astype(F32)
    for k in range(2, NZ):
        total += z_recv[k].astype(F32)
    mine = x_own[pl.ds(pl.multiple_of(z * 8, 8), 8), :]
    dgrad_ref[:, :384] = mine[:, :384] + total[:8]
    dgrad_ref[:, 384:] = mine[:, 384:] + total[8:]

    for one in sends:
        one.wait_send()


def body(states, inner_weights, down_weight, cotangent, routes):
    dma = lambda *shape: pltpu.SemaphoreType.DMA(shape)
    vm = lambda shape, kind=BF: pltpu.VMEM(shape, kind)
    return pl.pallas_call(
        kernel,
        out_shape=(
            jax.ShapeDtypeStruct((TOK, DW // NY), BF),
            jax.ShapeDtypeStruct((TOK, HID), BF),
            jax.ShapeDtypeStruct((TOK, HID), BF),
            jax.ShapeDtypeStruct((DW // 128, HID), F32),
        ),
        in_specs=[pl.BlockSpec(memory_space=pl.ANY)] * 5,
        out_specs=tuple(pl.BlockSpec(memory_space=pltpu.VMEM) for _ in range(4)),
        scratch_shapes=[
            vm((1, TOK), jnp.int32),
            vm((TOK, D)),
            vm((2, 16, HID)),
            vm((8, HID)),
            vm((TOK, DW)),
            dma(5),
            vm((2, D, HID)),
            vm((DW, HID)),
            vm((8, HID)),
            vm((PIECES, NZ, 16, TILE)),
            vm((PIECES, NZ, 16, TILE)),
            vm((PIECES, NQ, 32, TILE)),
            vm((PIECES, NQ, 32, TILE)),
            vm((PIECES, NY, TOK, TILE)),
            vm((TOK, HID)),
            vm((DW, TOK), F32),
            vm((DW, TOK), F32),
            vm((DW, TOK)),
            vm((DW // 2, HID)),
            vm((DW // 2, HID)),
            vm((DW // 2, HID), F32),
            vm((NX, 128, HID)),
            vm((NX, 128, HID)),
            vm((128, HID), F32),
            vm((NZ, 16, HID // 2)),
            vm((NZ, 16, HID // 2)),
            vm((NY, TOK, DW // NY)),
            vm((NY, TOK, DW // NY)),
            dma(2),
            dma(2),
        ]
        + [dma(NZ)] * 10
        + [dma(3), dma(3)]
        + [dma(NZ)] * 4
        + [dma(PIECES, NZ)] * 2
        + [dma(PIECES, NQ)] * 2
        + [dma(PIECES, NY)] * 2
        + [dma(1), dma(1), dma(NX), dma(NX), dma(NZ), dma(NZ), dma(NY), dma(NY)],
        compiler_params=pltpu.CompilerParams(
            collective_id=0, has_side_effects=True, vmem_limit_bytes=60 * 1024 * 1024
        ),
    )(routes.reshape(1, TOK), states, inner_weights, down_weight, cotangent)


def solution(mesh):
    return jax.shard_map(
        body,
        mesh=mesh,
        in_specs=(P("dp", None), P(None, "dp", "mp"), P("dp", "mp"), P("dp", None), P("dp")),
        out_specs=(P("dp", "mp"), P("dp", "mp"), P("dp", "mp"), P("dp", "mp")),
        check_vma=False,
    )
```

```python
import jax
import jax.numpy as jnp
from jax import lax
from jax.experimental import pallas as pl
from jax.experimental.pallas import tpu as pltpu
from jax.sharding import PartitionSpec as P

BF = jnp.bfloat16
F32 = jnp.float32
MESH = pl.DeviceIdType.MESH

NZ, NX, NY = 16, 4, 4
NQ = NX * 2
TOK = 256
D = 2048
HID = 768
DW = 1024
SQ = D // NY
CQ = DW // NY
TILE = 256

ORDER = (0, -1, 1, -2, 2, -3, 3, -4, 4, -5, 5, -6, 6, -7, 7, 8)
NEXT = {0: ((1, -1), (-1, 1)), -7: ((1, 8),)}
for _k in range(1, 7):
    NEXT[-_k] = ((1, -_k - 1),)
    NEXT[_k] = ((-1, _k + 1),)
PIECES = 3
AT_Q, AT_Y = (10, 15, 20), (15, 20, 21)
PER_STEP = 3
FAR = [k for j in range(1, NZ // 2) for k in (j, NZ - j)] + [NZ // 2]
TURN = 4
LAGX = 2
LAGS = 4
LAGD = 3
LAST = NZ + 4
BATCH = 4
AT_ADD = (10, 14, 18)


def goes_right(i):
    return ORDER[i] <= 0


def kernel(
    routes_in, states_in, inner_in, down_in, cot_in,
    layer_ref, gates_ref, linear_ref, dgrad_ref,
    routes_ref, states_ref, inner_ref, down_ref, cot_ref, in_sem,
    w, dn, dsib, s_buf, r1, t_buf, r2, rows, hidden, ct, ctp32, ctp,
    p_send, p_recv, p_own, x_send, x_recv, x_own, z_send, z_recv, l_send, l_recv,
    acc, sib0_s, sib0_r, zs, zr, xls, xlr, xrs, xrr, x2s, x2r, sbs, sbr, dxs, dxr, dzs, dzr, dss, dsr,
    a1s, a1r, a2s, a2r, a3s, a3r, p0s, p0r, p1s, p1r, p2s, p2r, ls, lr,
):
    d, y = lax.axis_index("dp"), lax.axis_index("mp")
    c, x, z = lax.rem(d, 2), lax.rem(d // 2, NX), d // NQ
    q = lax.rem(d, NQ)

    def dev(zz, xx, cc):
        return ((zz * NX + xx) * 2 + cc, y)

    def plus(a, k, n):
        return lax.rem(a + (k + n), n)

    def remote(src, dst, send, recv, to):
        return pltpu.make_async_remote_copy(
            src_ref=src, dst_ref=dst, send_sem=send, recv_sem=recv, device_id=to, device_id_type=MESH
        )

    right, left = dev(z, plus(x, 1, NX), c), dev(z, plus(x, -1, NX), c)
    sibling = dev(z, x, 1 - c)

    pairs = (
        (inner_in, inner_ref),
        (down_in, down_ref),
        (routes_in, routes_ref),
        (states_in, states_ref),
        (cot_in, cot_ref),
    )
    loads = [pltpu.make_async_copy(a, b, in_sem.at[i]) for i, (a, b) in enumerate(pairs)]
    for one in loads:
        one.start()

    barrier = pltpu.get_barrier_semaphore()
    for k in range(1, NZ):
        pl.semaphore_signal(barrier, inc=1, device_id=dev(plus(z, k, NZ), x, c), device_id_type=MESH)
    for k in range(1, NQ):
        qq = plus(q, k, NQ)
        pl.semaphore_signal(barrier, inc=1, device_id=(z * NQ + qq, y), device_id_type=MESH)
    for k in range(1, NY):
        pl.semaphore_signal(barrier, inc=1, device_id=(d, plus(y, k, NY)), device_id_type=MESH)
    pl.semaphore_wait(barrier, NZ + NQ + NY - 3)

    def chunk(zz, xx, lane):
        return w.at[lane, pl.ds(pl.multiple_of((zz * NX + xx) * 32, 32), 32), :]

    def group(zz, lane):
        return w.at[lane, pl.ds(pl.multiple_of(zz * 128, 128), 128), :]

    def lanes(lane):
        return pl.ds(pl.multiple_of(lane * 384, 128), 384)

    def down_chunk(xx):
        return dn.at[pl.ds(pl.multiple_of((z * NX + xx) * 16, 16), 16), lanes(c)]

    def down_group(zz, lane):
        return dn.at[pl.ds(pl.multiple_of(zz * 64, 64), 64), lanes(lane)]

    def move(ref, send, recv, i, to):
        return [remote(ref, ref, send.at[i], recv.at[i], to)]

    sends = []

    def start(copies):
        for one in copies:
            one.start()
        sends.extend(copies)

    def arrive(copies):
        for one in copies:
            one.wait_recv()

    loads[0].wait()
    loads[1].wait()
    own_row = pl.multiple_of((z * NX + x) * 32 + c * 16, 16)
    sib_copies = [
        remote(
            inner_ref.at[1 - c], w.at[1 - c, pl.ds(own_row, 16), :], sib0_s.at[0], sib0_r.at[0], sibling
        ),
        remote(down_ref, dsib, sib0_s.at[1], sib0_r.at[1], sibling),
    ]
    start(sib_copies)
    w[c, pl.ds(own_row, 16), :] = inner_ref[c]

    for one in loads[2:]:
        one.wait()
    r_row = jnp.broadcast_to(routes_ref[...].astype(F32), (TOK, TOK))
    r_col = r_row.T
    sub = lax.broadcasted_iota(jnp.int32, (TOK, TOK), 0)
    lane_i = lax.broadcasted_iota(jnp.int32, (TOK, TOK), 1)
    before = jnp.where((r_row == r_col) & (sub < lane_i), 1.0, 0.0)
    count = jnp.sum(before, axis=0, keepdims=True)
    slot = jnp.where(r_row >= 0, r_row * 2.0 + count, -1.0)
    pick = jnp.where(slot == sub.astype(F32), 1.0, 0.0).astype(BF)
    for p in range(PIECES):
        if p < 2:
            values = states_ref[:, pl.ds(pl.multiple_of(y * SQ + p * TILE, TILE), TILE)]
        else:
            values = cot_ref[:, pl.ds(pl.multiple_of(y * CQ, CQ), CQ)]
        part = jnp.dot(pick, values, preferred_element_type=F32).astype(BF)
        s_buf[p] = part.reshape(NZ, 16, TILE)
        r1[p, pl.ds(z, 1)] = s_buf[p, pl.ds(z, 1)]

    theirs = [
        remote(
            inner_ref.at[c],
            w.at[c, pl.ds(pl.multiple_of((z * NX + x) * 32 + (1 - c) * 16, 16), 16), :],
            sib0_s.at[0],
            sib0_r.at[0],
            sibling,
        ),
        sib_copies[1],
    ]
    arrive(theirs)
    mine32, sib32 = down_ref[...].astype(F32), dsib[...].astype(F32)
    first, second = jnp.where(c == 0, mine32, sib32), jnp.where(c == 0, sib32, mine32)
    both = jnp.concatenate([first, second], axis=0)
    both = jnp.where(c == 0, both[:, :384], both[:, 384:]).astype(BF)
    dn[pl.ds(pl.multiple_of((z * NX + x) * 16, 16), 16), lanes(c)] = both

    def send_z(ref, send, recv, i):
        for step, there in NEXT.get(ORDER[i], ()):
            start(move(ref, send, recv, ORDER.index(there), dev(plus(z, step, NZ), x, c)))

    def send_x(i):
        own = chunk(plus(z, ORDER[i], NZ), x, c)
        start(move(own, xls, xlr, i, right))
        start(move(own, xrs, xrr, i, left))

    def pass_x(i):
        zz = plus(z, ORDER[i], NZ)
        from_left, from_right = chunk(zz, plus(x, -1, NX), c), chunk(zz, plus(x, 1, NX), c)
        arrive(move(from_left, xls, xlr, i, right))
        arrive(move(from_right, xrs, xrr, i, left))
        if goes_right(i):
            start(move(from_left, x2s, x2r, i, right))
        else:
            start(move(from_right, x2s, x2r, i, left))

    def to_sibling(i):
        zz = plus(z, ORDER[i], NZ)
        arrive(move(chunk(zz, plus(x, 2, NX), c), x2s, x2r, i, right))
        start(move(group(zz, c), sbs, sbr, i, sibling))

    onward = 1 - 2 * c

    def down_x():
        start(move(down_chunk(x), dxs, dxr, 0, right))
        start(move(down_chunk(x), dxs, dxr, 1, left))

    def down_x2():
        arrive(move(down_chunk(plus(x, -1, NX)), dxs, dxr, 0, right))
        arrive(move(down_chunk(plus(x, 1, NX)), dxs, dxr, 1, left))
        start(move(down_chunk(plus(x, -onward, NX)), dxs, dxr, 2, dev(z, plus(x, onward, NX), c)))

    def down_z(i):
        ref = down_group(plus(z, ORDER[i], NZ), c)
        if i == 0:
            arrive(move(down_chunk(plus(x, 2, NX)), dxs, dxr, 2, right))
        else:
            arrive(move(ref, dzs, dzr, i, right))
        send_z(ref, dzs, dzr, i)
        start(move(ref, dss, dsr, i, sibling))

    def rows_z(i):
        for n in range(i * PER_STEP, min((i + 1) * PER_STEP, PIECES * (NZ - 1))):
            p, k = n // (NZ - 1), FAR[n % (NZ - 1)]
            to = plus(z, k, NZ)
            start([remote(s_buf.at[p, to], r1.at[p, z], a1s.at[p, k], a1r.at[p, k], dev(to, x, c))])

    def permuted(values, out_first):
        low = sub % out_first
        src = (low // 2) * (TOK // (out_first // 2)) + (sub // out_first) * 2 + sub % 2
        matrix = jnp.where(src == lane_i, 1.0, 0.0).astype(BF)
        return jnp.dot(matrix, values, preferred_element_type=F32).astype(BF)

    def rows_q(p):
        for k in range(1, NZ):
            at = plus(z, -k, NZ)
            arrive([remote(s_buf.at[p, at], r1.at[p, at], a1s.at[p, k], a1r.at[p, k], dev(at, x, c))])
        t_buf[p] = permuted(r1[p].reshape(TOK, TILE), 32).reshape(NQ, 32, TILE)
        r2[p, pl.ds(q, 1)] = t_buf[p, pl.ds(q, 1)]
        for k in range(1, NQ):
            to = plus(q, k, NQ)
            start([remote(t_buf.at[p, to], r2.at[p, q], a2s.at[p, k], a2r.at[p, k], (z * NQ + to, y))])

    def rows_y(p):
        for k in range(1, NQ):
            at = plus(q, -k, NQ)
            arrive([remote(t_buf.at[p, at], r2.at[p, at], a2s.at[p, k], a2r.at[p, k], (z * NQ + at, y))])
        rows[p, pl.ds(y, 1)] = permuted(r2[p].reshape(TOK, TILE), 16).reshape(1, TOK, TILE)
        for k in range(1, NY):
            mine = rows.at[p, y]
            start([remote(mine, mine, a3s.at[p, k], a3r.at[p, k], (d, plus(y, k, NY)))])

    def columns(t):
        if isinstance(t, int):
            return slice(t * TILE, (t + 1) * TILE)
        return pl.ds(pl.multiple_of(t * TILE, TILE), TILE)

    def group_product(n, lane, cols):
        total = None
        for i in range(n * BATCH, (n + 1) * BATCH):
            at = pl.ds(pl.multiple_of(plus(z, ORDER[i], NZ) * 128, 128), 128)
            one = jnp.dot(states_ref[:, at], w[lane, at, cols], preferred_element_type=F32)
            total = one if total is None else total + one
        return total

    def groups_arrive(n):
        for i in range(n * BATCH, (n + 1) * BATCH):
            arrive(move(group(plus(z, ORDER[i], NZ), 1 - c), sbs, sbr, i, sibling))

    def add_groups(n):
        groups_arrive(n)

        def one(t, carry):
            cols = columns(t)
            for lane in range(2):
                more = group_product(n, lane, cols)
                acc[lane, :, cols] = more if n == 0 else acc[lane, :, cols] + more
            return carry

        lax.fori_loop(0, HID // TILE, one, 0)

    def rows_step(i):
        if i in AT_Q:
            rows_q(AT_Q.index(i))
        if i in AT_Y:
            rows_y(AT_Y.index(i))

    def rows_done():
        for p in range(PIECES):
            for k in range(1, NY):
                at = plus(y, -k, NY)
                arrive([remote(rows.at[p, at], rows.at[p, at], a3s.at[p, k], a3r.at[p, k], (d, at))])

    def transpose_cot():
        keep = r_col >= 0
        for j in range(DW // TILE):
            cols = slice(j * TILE, (j + 1) * TILE)
            ct[cols, :] = jnp.where(keep, cot_ref[:, cols].astype(F32), 0.0).T

        def one(n, carry):
            zz, xx, cc = n // NQ, (n // 2) % NX, n % 2
            to = (cc * NX + xx) * NZ + zz
            ctp32[pl.ds(pl.multiple_of(to * 8, 8), 8), :] = ct[pl.ds(pl.multiple_of(n * 8, 8), 8), :]
            return carry

        lax.fori_loop(0, NZ * NQ, one, 0)
        ctp[...] = ctp32[...].astype(BF)

    for i in range(LAST):
        if i < NZ:
            ref = chunk(plus(z, ORDER[i], NZ), x, c)
            if i > 0:
                arrive(move(ref, zs, zr, i, right))
            send_z(ref, zs, zr, i)
            send_x(i)
        if i == 0:
            down_x()
        if i == 1:
            down_x2()
        rows_z(i)
        if 0 <= i - LAGX < NZ:
            pass_x(i - LAGX)
        if 0 <= i - LAGD < NZ:
            down_z(i - LAGD)
        if 0 <= i - LAGS < NZ:
            to_sibling(i - LAGS)
        if i == TURN:
            transpose_cot()
        rows_step(i)
        if i in AT_ADD:
            add_groups(AT_ADD.index(i))
    groups_arrive(NZ // BATCH - 1)

    rows_step(LAST)

    def preacts(gate_f32, up_f32):
        gate = gate_f32.astype(BF).astype(F32)
        up_value = up_f32.astype(BF).astype(F32)
        sig = jax.nn.sigmoid(gate)
        return gate, up_value, sig, gate * sig

    def forward(t, carry):
        cols = columns(t)
        _, up_value, _, active = preacts(
            acc[0, :, cols] + group_product(NZ // BATCH - 1, 0, cols),
            acc[1, :, cols] + group_product(NZ // BATCH - 1, 1, cols),
        )
        hidden[:, cols] = (active * up_value).astype(BF)
        return carry

    half = DW // 2
    tiles = range(HID // TILE)

    def product(t, first_row, m):
        at = pl.multiple_of(first_row + m * TILE, TILE)
        return jnp.dot(ctp[pl.ds(at, TILE), :], hidden[:, columns(t)], preferred_element_type=F32)

    def core_send(t):
        for m in range(half // TILE):
            p_send[t, m * TILE : (m + 1) * TILE, :] = product(t, (1 - c) * half, m).astype(BF)
        start([remote(p_send.at[t], p_recv.at[t], p0s.at[t], p0r.at[t], sibling)])
        for m in range(half // TILE):
            p_own[t, m * TILE : (m + 1) * TILE, :] = product(t, c * half, m)

    def x_copy(t, k):
        to = dev(z, plus(x, k, NX), c)
        return remote(x_send.at[t, k], x_recv.at[t, k], p1s.at[t, k], p1r.at[t, k], to)

    def x_sends(t):
        arrive([remote(p_send.at[t], p_recv.at[t], p0s.at[t], p0r.at[t], sibling)])
        for k in (2, 1, 3):
            at = pl.ds(pl.multiple_of(plus(x, k, NX) * 128, 128), 128)
            x_send[t, k] = (p_own[t, at, :] + p_recv[t, at, :].astype(F32)).astype(BF)
            start([x_copy(t, k)])
        at = pl.ds(pl.multiple_of(x * 128, 128), 128)
        x_own[t] = p_own[t, at, :] + p_recv[t, at, :].astype(F32)

    def z_copy(t, k):
        to = plus(z, k, NZ)
        return remote(z_send.at[t, to], z_recv.at[t, k], p2s.at[t, k], p2r.at[t, k], dev(to, x, c))

    def z_sends(t):
        arrive([x_copy(t, k) for k in range(1, NX)])
        total = x_own[t]
        for k in range(1, NX):
            total += x_recv[t, k].astype(F32)
        x_own[t] = total
        pieces = total.reshape(NZ, 8, TILE)
        z_send[t] = jnp.concatenate([pieces[:, :, :128], pieces[:, :, 128:]], axis=1).astype(BF)
        start([z_copy(t, k) for k in FAR])

    forward(0, 0)
    core_send(0)
    forward(1, 0)
    core_send(1)
    x_sends(0)
    rows_step(LAST + 1)
    forward(2, 0)
    core_send(2)
    x_sends(1)

    for i in range(NZ):
        arrive(move(down_group(plus(z, ORDER[i], NZ), 1 - c), dss, dsr, i, sibling))

    def layer_part(yy):
        return lax.dot_general(
            hidden[...],
            dn[pl.ds(pl.multiple_of(yy * TILE, TILE), TILE), :],
            (((1,), (1,)), ((), ())),
            preferred_element_type=F32,
        ).astype(BF)

    x_sends(2)
    layer_copies = []
    for k in range(1, NY):
        to = plus(y, k, NY)
        l_send[k] = layer_part(to)
        layer_copies.append(remote(l_send.at[k], l_recv.at[k], ls.at[k], lr.at[k], (d, to)))
        start(layer_copies[-1:])
    rows_step(LAST + 2)
    z_sends(0)
    l_send[0] = layer_part(y)
    rows_step(LAST + 3)
    z_sends(1)
    z_sends(2)
    rows_step(LAST + 4)

    rows_done()

    def backward(t, carry):
        cols = columns(t)
        gate = jnp.zeros((TOK, TILE), F32)
        up_value = jnp.zeros((TOK, TILE), F32)
        d_hidden = jnp.zeros((TOK, TILE), F32)
        for yy in range(NY):
            for p in range(2):
                at = slice(yy * SQ + p * TILE, yy * SQ + (p + 1) * TILE)
                gate += jnp.dot(rows[p, yy], w[0, at, cols], preferred_element_type=F32)
                up_value += jnp.dot(rows[p, yy], w[1, at, cols], preferred_element_type=F32)
            at = slice(yy * CQ, (yy + 1) * CQ)
            d_hidden += jnp.dot(rows[2, yy], dn[at, cols], preferred_element_type=F32)
        gate, up_value, sig, active = preacts(gate, up_value)
        gates_ref[:, cols] = (d_hidden * up_value * (sig * (1.0 + gate * (1.0 - sig)))).astype(BF)
        linear_ref[:, cols] = (d_hidden * active).astype(BF)
        return carry

    lax.fori_loop(0, HID // TILE, backward, 0)

    arrive(layer_copies)
    layer_ref[...] = (
        l_send[0].astype(F32)
        + l_recv[1].astype(F32)
        + l_recv[2].astype(F32)
        + l_recv[3].astype(F32)
    ).astype(BF)

    for t in tiles:
        arrive([z_copy(t, k) for k in FAR])
        total = z_recv[t, 1].astype(F32)
        for k in range(2, NZ):
            total += z_recv[t, k].astype(F32)
        mine = x_own[t, pl.ds(pl.multiple_of(z * 8, 8), 8), :]
        dgrad_ref[:, t * TILE : t * TILE + 128] = mine[:, :128] + total[:8]
        dgrad_ref[:, t * TILE + 128 : (t + 1) * TILE] = mine[:, 128:] + total[8:]

    for one in sends:
        one.wait_send()


def body(states, inner_weights, down_weight, cotangent, routes):
    dma = lambda *shape: pltpu.SemaphoreType.DMA(shape)
    vm = lambda shape, kind=BF: pltpu.VMEM(shape, kind)
    return pl.pallas_call(
        kernel,
        out_shape=(
            jax.ShapeDtypeStruct((TOK, DW // NY), BF),
            jax.ShapeDtypeStruct((TOK, HID), BF),
            jax.ShapeDtypeStruct((TOK, HID), BF),
            jax.ShapeDtypeStruct((DW // 128, HID), F32),
        ),
        in_specs=[pl.BlockSpec(memory_space=pl.ANY)] * 5,
        out_specs=tuple(pl.BlockSpec(memory_space=pltpu.VMEM) for _ in range(4)),
        scratch_shapes=[
            vm((1, TOK), jnp.int32),
            vm((TOK, D)),
            vm((2, 16, HID)),
            vm((8, HID)),
            vm((TOK, DW)),
            dma(5),
            vm((2, D, HID)),
            vm((DW, HID)),
            vm((8, HID)),
            vm((PIECES, NZ, 16, TILE)),
            vm((PIECES, NZ, 16, TILE)),
            vm((PIECES, NQ, 32, TILE)),
            vm((PIECES, NQ, 32, TILE)),
            vm((PIECES, NY, TOK, TILE)),
            vm((TOK, HID)),
            vm((DW, TOK), F32),
            vm((DW, TOK), F32),
            vm((DW, TOK)),
            vm((HID // TILE, DW // 2, TILE)),
            vm((HID // TILE, DW // 2, TILE)),
            vm((HID // TILE, DW // 2, TILE), F32),
            vm((HID // TILE, NX, 128, TILE)),
            vm((HID // TILE, NX, 128, TILE)),
            vm((HID // TILE, 128, TILE), F32),
            vm((HID // TILE, NZ, 16, 128)),
            vm((HID // TILE, NZ, 16, 128)),
            vm((NY, TOK, DW // NY)),
            vm((NY, TOK, DW // NY)),
            vm((2, TOK, HID), F32),
            dma(2),
            dma(2),
        ]
        + [dma(NZ)] * 10
        + [dma(3), dma(3)]
        + [dma(NZ)] * 4
        + [dma(PIECES, NZ)] * 2
        + [dma(PIECES, NQ)] * 2
        + [dma(PIECES, NY)] * 2
        + [dma(3), dma(3), dma(3, NX), dma(3, NX), dma(3, NZ), dma(3, NZ), dma(NY), dma(NY)],
        compiler_params=pltpu.CompilerParams(
            collective_id=0, has_side_effects=True, vmem_limit_bytes=60 * 1024 * 1024
        ),
    )(routes.reshape(1, TOK), states, inner_weights, down_weight, cotangent)


def solution(mesh):
    return jax.shard_map(
        body,
        mesh=mesh,
        in_specs=(P("dp", None), P(None, "dp", "mp"), P("dp", "mp"), P("dp", None), P("dp")),
        out_specs=(P("dp", "mp"), P("dp", "mp"), P("dp", "mp"), P("dp", "mp")),
        check_vma=False,
    )
```
